32 devices in a mesh: dp: 8 (over y, x, core), tensor: 4 (over z).
Axes of the slice: x: 2, y: 2, z: 4, core: 2. Of those that a mesh axis runs over, the one named last changes fastest.
Arguments:
- tokens: bfloat16 [2048, 8192], P('dp', 'tensor'), may hold values from -160 to 160
- weights: bfloat16 [3, 512, 32, 256], P(None, None, 'tensor'), may hold values from -0.25 to 0.25
- cotangent: bfloat16 [2048, 8192], P('dp', 'tensor'), may hold values from -6 to 6
Outputs:
- mixed: bfloat16 [2048, 8192], P('dp', 'tensor')
- token_grads: bfloat16 [2048, 8192], P('dp', 'tensor')
- weight_grads: float32 [3, 512, 32, 256], P(None, 'dp', 'tensor')
The draws below stay inside these ranges and needn't reach their ends.
All inputs are finite; a program needn't handle non-finite values.
Results may differ from the reference program's by a relative error of at most 0.0014.
The reference program's roundings to bfloat16 on the way count: a program that leaves them out, or rounds other values in their place, can miss the bound.
Values may be sent and summed in bfloat16 or wider, within the bound.
A program may use at most 128 MiB of HBM per device.

```python
import math
import jax
import jax.numpy as jnp
from jax import lax

D = 8192
BLK = 256
FACTORS = 3
TOK_DEV = 256
NBLK = 32
TOKENS = 2048
N_DP = 8


def draw_tokens(key, part):
    key_base, key_rows, key_cols = jax.random.split(key, 3)
    cols = jnp.exp(jax.random.uniform(key_cols, (1, D), jnp.float32, 0.0, math.log(10.0)))
    trend = jnp.exp(math.log(3.0) * jnp.arange(D, dtype=jnp.float32) / D)[None, :]
    rows = jnp.exp(jax.random.uniform(key_rows, (TOKENS, 1), jnp.float32, 0.0, math.log(10.0)))
    base = jnp.clip(jax.random.normal(key_base, (TOKENS, D), jnp.float32), -4.0, 4.0)
    return (base * rows * cols * trend * 0.1).astype(jnp.bfloat16)


def shard_levels(rng, dims, shards, smallest, top_value):
    def one(axis_at, parts):
        draws = jax.random.uniform(jax.random.fold_in(jax.random.fold_in(rng, 6), axis_at), (parts,), jnp.float32, smallest / len(shards), top_value / len(shards))
        return jnp.repeat(jnp.exp(draws), dims[axis_at] // parts).reshape((-1,) + (1,) * (len(dims) - axis_at - 1))

    gain = one(*shards[0])
    for cut in shards[1:]:
        gain = gain * one(*cut)
    return gain


def bell_draw(rng, dims, spread, most, cuts=(), kind=jnp.bfloat16):
    drawn = spread * jax.random.normal(rng, dims, jnp.float32)
    if cuts:
        drawn = drawn * shard_levels(rng, dims, cuts, -0.22, 0.18)
    return jnp.clip(drawn, -most, most).astype(kind)


def setup_inputs(seed: int = 0) -> dict:
    keys = jax.random.split(jax.random.key(seed), 4)
    tokens = draw_tokens(jax.random.fold_in(keys[3], 71), 0)
    weights = bell_draw(keys[1], (FACTORS, 2 * BLK, NBLK, BLK), (2 * BLK) ** -0.5, 0.25, ((2, 4),))
    cotangent = bell_draw(keys[2], (TOKENS, D), 1.0, 6.0, ((0, 8), (1, 4)))
    return {"tokens": tokens, "weights": weights, "cotangent": cotangent}


root_half = 0.7071067811865476
pdf_scale = 0.3989422804014327
epsilon = 1e-06

def gelu_value(value):
    return value * (0.5 * (1.0 + lax.erf(value * root_half)))

def gelu_slope(value):
    return 0.5 * (1.0 + lax.erf(value * root_half)) + value * jnp.exp(-0.5 * value * value) * pdf_scale

def local_partner(blocks, stride):
    tok_rows, block_count, width = blocks.shape
    folded = blocks.reshape(tok_rows, block_count // (2 * stride), 2, stride, width)
    return jnp.flip(folded, axis=2).reshape(tok_rows, block_count, width)

def layer_pass(tok_block, cot_block, weights_f32, block_bits):
    tok_rows = tok_block.shape[0]
    tokens_f32 = tok_block.astype(jnp.float32)
    square_sum = lax.optimization_barrier(jnp.sum(tokens_f32 * tokens_f32, axis=1))
    inv_rms = lax.rsqrt(square_sum / D + epsilon)[:, None]
    normed = tokens_f32 * inv_rms
    hidden = normed.astype(jnp.bfloat16).reshape(tok_rows, NBLK, BLK)
    stored_inputs = []
    stored_preact = []
    preact = None
    for factor in range(FACTORS):
        stride = 1 << block_bits - FACTORS + factor
        partner = local_partner(hidden, stride)
        layer_weights = weights_f32[factor]
        preact = jnp.einsum('tbc,cbd->tbd', hidden.astype(jnp.float32), layer_weights[:BLK])
        preact = preact + jnp.einsum('tbc,cbd->tbd', partner.astype(jnp.float32), layer_weights[BLK:])
        stored_inputs.append((hidden, partner))
        stored_preact.append(preact)
        if factor < FACTORS - 1:
            hidden = gelu_value(preact).astype(jnp.bfloat16)
    mixed = (tokens_f32 + preact.reshape(tok_rows, D)).astype(jnp.bfloat16)
    grad_pre = cot_block.reshape(tok_rows, NBLK, BLK)
    grad_terms = []
    grad_hidden = None
    for factor in reversed(range(FACTORS)):
        stride = 1 << block_bits - FACTORS + factor
        hidden, partner = stored_inputs[factor]
        joined = jnp.concatenate([hidden, partner], axis=2).astype(jnp.float32)
        grad_f32 = grad_pre.astype(jnp.float32)
        grad_terms.append(jnp.einsum('tbc,tbd->cbd', joined, grad_f32))
        layer_weights = weights_f32[factor]
        near_term = jnp.einsum('tbd,cbd->tbc', grad_f32, layer_weights[:BLK])
        far_term = jnp.einsum('tbd,cbd->tbc', grad_f32, layer_weights[BLK:])
        grad_hidden = near_term + local_partner(far_term, stride)
        if factor > 0:
            grad_pre = (grad_hidden * gelu_slope(stored_preact[factor - 1])).astype(jnp.bfloat16)
    flat = grad_hidden.reshape(tok_rows, D)
    inner_sum = lax.optimization_barrier(jnp.sum(flat * normed, axis=1))
    token_grads = (cot_block.astype(jnp.float32) + inv_rms * (flat - normed * (inner_sum / D)[:, None])).astype(jnp.bfloat16)
    return (mixed, token_grads, jnp.stack(grad_terms[::-1]))

def reference(tokens, weights, cotangent):
    block_bits = NBLK.bit_length() - 1
    weights_f32 = weights.astype(jnp.float32)
    tok_groups = tokens.reshape(N_DP, TOK_DEV, D)
    cot_groups = cotangent.reshape(N_DP, TOK_DEV, D)

    def one_group(totals, pair):
        tok_block, cot_block = pair
        mixed, token_grads, grad_terms = layer_pass(tok_block, cot_block, weights_f32, block_bits)
        return (totals + grad_terms, (mixed, token_grads))
    initial = jnp.zeros((FACTORS, 2 * BLK, NBLK, BLK), jnp.float32)
    totals, outputs = lax.scan(one_group, initial, (tok_groups, cot_groups))
    mixed, token_grads = outputs
    weight_grads = totals * (1.0 / math.sqrt(TOKENS))
    return (mixed.reshape(TOKENS, D), token_grads.reshape(TOKENS, D), weight_grads)
```

```python
import functools
import math

import jax
import jax.numpy as jnp
from jax import lax
from jax.experimental import pallas as pl
from jax.experimental.pallas import tpu as pltpu
from jax.sharding import PartitionSpec as P

D = 8192
BLK = 256
FACTORS = 3
CH = 4

root_half = 0.7071067811865476
pdf_scale = 0.3989422804014327
epsilon = 1e-06
MESH = pl.DeviceIdType.MESH
F32 = jnp.float32
BF16 = jnp.bfloat16


def nn(a, b):
    return lax.dot_general(a, b, (((1,), (0,)), ((), ())), preferred_element_type=F32)


def nt(a, b):
    return lax.dot_general(a, b, (((1,), (1,)), ((), ())), preferred_element_type=F32)


def tn(a, b):
    return lax.dot_general(a, b, (((0,), (0,)), ((), ())), preferred_element_type=F32)


def gelu_and_slope(value):
    cdf = 0.5 * (1.0 + lax.erf(value * root_half))
    return value * cdf, cdf + value * jnp.exp(-0.5 * value * value) * pdf_scale


def kernel(
    n_dp, n_z, tok, cot, wt, mixed, tg, wg,
    W, Wfp, cotp, h0, h1, h1p, h2, h2p, g1, g1p, sl0, sl1, dh0, acc, invr,
    A, R0, R1a, R1b, R2a, R2b, stat,
    wsem, st_s, st_r, wz_s, wz_r, wb_s, wb_r, ct_s, ct_r,
    h1_s, h1_r, h2_s, h2_r, g1_s, g1_r,
    s0_s, s0_r, s1a_s, s1a_r, s1b_s, s1b_r, s2a_s, s2a_r, s2b_s, s2b_r,
):
    na = n_dp // 4
    rows = 2 * BLK // n_dp
    wrows = 8 * BLK // n_dp
    per_block = n_dp // 8
    d = lax.axis_index("dp")
    z = lax.axis_index("tensor")
    da = d // 4
    dx = (d // 2) % 2
    dc = d % 2
    grad_scale = 1.0 / math.sqrt(tok.shape[0] * n_dp)
    tok_rows = tok.shape[0]

    def xor(v, o):
        out = v
        bit = 1
        while bit <= o:
            if o & bit:
                out = out + bit - 2 * bit * ((v // bit) % 2)
            bit *= 2
        return out

    zp = {1: xor(z, 1), 2: xor(z, 2)}

    def remote(src, dst, s, r, where):
        return pltpu.make_async_remote_copy(
            src_ref=src, dst_ref=dst, send_sem=s, recv_sem=r,
            device_id=where, device_id_type=MESH,
        )

    wload = pltpu.make_async_copy(wt, W, wsem)
    wload.start()

    def stat_copy(which, o):
        return remote(
            stat.at[which, z], stat.at[which, z],
            st_s.at[which, o - 1], st_r.at[which, o - 1], {"tensor": xor(z, o)},
        )

    def stat_arrival(which, o):
        zo = xor(z, o)
        return remote(
            stat.at[which, zo], stat.at[which, zo],
            st_s.at[which, o - 1], st_r.at[which, o - 1], {"tensor": zo},
        )

    def put_stat(which, column):
        wide = jnp.broadcast_to(column, (tok_rows, 128))
        stat[which, z] = jnp.transpose(wide)[0:8]

    def get_stat(which):
        total = stat[which, 0]
        for i in range(1, n_z):
            total = total + stat[which, i]
        wide = jnp.broadcast_to(total[0:1], (128, tok_rows))
        return jnp.transpose(wide)[:, 0:1]

    part = jnp.zeros((tok_rows, BLK), F32)
    for i in range(2 * CH):
        x = tok[:, i * BLK:(i + 1) * BLK].astype(F32)
        part = part + x * x
    put_stat(0, jnp.sum(part, axis=1, keepdims=True))

    barrier = pltpu.get_barrier_semaphore()
    for o in range(1, n_z):
        pl.semaphore_signal(barrier, inc=1, device_id={"tensor": xor(z, o)}, device_id_type=MESH)
    for o in range(1, n_dp):
        pl.semaphore_signal(barrier, inc=1, device_id={"dp": xor(d, o)}, device_id_type=MESH)
    pl.semaphore_wait(barrier, n_z + n_dp - 2)

    for o in range(1, n_z):
        stat_copy(0, o).start()

    def far_weights(k):
        return remote(
            wt.at[k, d // per_block,
                  pl.ds(pl.multiple_of(BLK + (d % per_block) * wrows, wrows), wrows)],
            Wfp.at[k - 1, d], wz_s.at[k - 1], wz_r.at[k - 1], {"tensor": zp[k]},
        )

    far_weights(2).start()
    far_weights(1).start()

    def cols(c, b):
        return pl.ds(pl.multiple_of((c + CH * b) * BLK, BLK), BLK)

    def cot_copy(c, b):
        return remote(cot.at[:, cols(c, b)], cotp.at[c, b],
                      ct_s.at[c, b], ct_r.at[c, b], {"tensor": zp[2]})

    for c in range(CH):
        for b in range(2):
            cot_copy(c, b).start()

    def h1_copy(c):
        return remote(h1.at[c], h1p.at[c], h1_s.at[c], h1_r.at[c], {"tensor": zp[1]})

    def h2_copy(c):
        return remote(h2.at[c], h2p.at[c], h2_s.at[c], h2_r.at[c], {"tensor": zp[2]})

    def g1_copy(c):
        return remote(g1.at[c], g1p.at[c], g1_s.at[c], g1_r.at[c], {"tensor": zp[1]})

    def s0_copy(j):
        return remote(A.at[j, :, :, :, 1 - dc], R0.at[j], s0_s.at[j], s0_r.at[j],
                      {"dp": xor(d, 1)})

    def s1_copies(j):
        out = [remote(A.at[j, 0, :, 1 - dx, dc], R1a.at[j], s1a_s.at[j], s1a_r.at[j],
                      {"dp": xor(d, 2)})]
        for o in range(1, na):
            out.append(remote(A.at[j, 1, xor(da, o), :, dc], R1b.at[j, o - 1],
                              s1b_s.at[j, o - 1], s1b_r.at[j, o - 1], {"dp": xor(d, 4 * o)}))
        return out

    def s2_copies(j):
        out = [remote(A.at[j, 1, da, 1 - dx, dc], R2b.at[j], s2b_s.at[j], s2b_r.at[j],
                      {"dp": xor(d, 2)})]
        for o in range(1, na):
            out.append(remote(A.at[j, 0, xor(da, o), dx, dc], R2a.at[j, o - 1],
                              s2a_s.at[j, o - 1], s2a_r.at[j, o - 1], {"dp": xor(d, 4 * o)}))
        return out

    def rs_start(j):
        s0_copy(j).start()

    def rs_step1(j):
        s0_copy(j).wait_recv()
        A[j, :, :, :, dc] = A[j, :, :, :, dc] + R0[j]
        for copy in s1_copies(j):
            copy.start()

    def rs_step2(j):
        for copy in s1_copies(j):
            copy.wait_recv()
        A[j, 0, :, dx, dc] = A[j, 0, :, dx, dc] + R1a[j]
        total = A[j, 1, da, :, dc]
        for o in range(1, na):
            total = total + R1b[j, o - 1]
        A[j, 1, da, :, dc] = total
        for copy in s2_copies(j):
            copy.start()

    def rs_finish(k, c):
        j = CH * k + c
        for copy in s2_copies(j):
            copy.wait_recv()
        total = A[j, 0, da, dx, dc]
        for o in range(1, na):
            total = total + R2a[j, o - 1]
        wg[k, c] = total * grad_scale
        wg[k, c + CH] = (A[j, 1, da, dx, dc] + R2b[j]) * grad_scale

    def put_grads(j, b, near, far):
        A[j, b, 0:na // 2] = near.reshape(na // 2, 2, 2, rows, BLK)
        A[j, b, na // 2:na] = far.reshape(na // 2, 2, 2, rows, BLK)

    wload.wait()
    for o in range(1, n_z):
        stat_arrival(0, o).wait_recv()
    invr[...] = jnp.broadcast_to(lax.rsqrt(get_stat(0) / D + epsilon), (tok_rows, 128))

    def normed(c, b):
        return tok[:, cols(c, b)].astype(F32) * invr[:, 0:1]

    def loop(body):
        def step(c, carry):
            body(c)
            return carry
        lax.fori_loop(0, CH, step, 0)

    def phase0(c):
        for b in range(2):
            h0[c, b] = normed(c, b).astype(BF16)
        for b in range(2):
            i = c + CH * b
            pre = nn(h0[c, b], W[0, i, 0:BLK]) + nn(h0[c, 1 - b], W[0, i, BLK:2 * BLK])
            value, slope = gelu_and_slope(pre)
            h1[c, b] = value.astype(BF16)
            sl0[c, b] = slope
        h1_copy(c).start()

    loop(phase0)

    def spread(k, o):
        return remote(Wfp.at[k - 1, d], Wfp.at[k - 1, d],
                      wb_s.at[k - 1, o - 1], wb_r.at[k - 1, o - 1], {"dp": xor(d, o)})

    def spread_arrival(k, o):
        other = xor(d, o)
        return remote(Wfp.at[k - 1, other], Wfp.at[k - 1, other],
                      wb_s.at[k - 1, o - 1], wb_r.at[k - 1, o - 1], {"dp": other})

    for k in (2, 1):
        far_weights(k).wait_recv()
        for o in range(1, n_dp):
            spread(k, o).start()

    def far_block(k, i):
        return Wfp[k - 1, pl.ds(i * per_block, per_block)].reshape(BLK, BLK)

    for o in range(1, n_dp):
        spread_arrival(2, o).wait_recv()

    def phase1(c):
        h1_copy(c).wait_recv()
        for b in range(2):
            i = c + CH * b
            pre = nn(h1[c, b], W[1, i, 0:BLK]) + nn(h1p[c, b], W[1, i, BLK:2 * BLK])
            value, slope = gelu_and_slope(pre)
            h2[c, b] = value.astype(BF16)
            sl1[c, b] = slope
        h2_copy(c).start()
        for b in range(2):
            i = c + CH * b
            cot_copy(c, b).wait_recv()
            dh = nt(cot[:, cols(c, b)], W[2, i, 0:BLK]) + nt(cotp[c, b], far_block(2, i))
            g1[c, b] = (dh * sl1[c, b]).astype(BF16)
        g1_copy(c).start()
        for b in range(2):
            put_grads(CH + c, b, tn(h1[c, b], g1[c, b]), tn(h1p[c, b], g1[c, b]))
        rs_start(CH + c)

        @pl.when(c >= 1)
        def _():
            rs_step1(CH + c - 1)

    loop(phase1)
    rs_step1(CH + CH - 1)
    for o in range(1, n_dp):
        spread_arrival(1, o).wait_recv()
    acc[...] = jnp.zeros_like(acc)

    def phase2(c):
        rs_step2(CH + c)
        g1_copy(c).wait_recv()
        g0 = []
        for b in range(2):
            i = c + CH * b
            dh = nt(g1[c, b], W[1, i, 0:BLK]) + nt(g1p[c, b], far_block(1, i))
            g0.append((dh * sl0[c, b]).astype(BF16))
        for b in range(2):
            put_grads(c, b, tn(h0[c, b], g0[b]), tn(h0[c, 1 - b], g0[b]))
        rs_start(c)
        for b in range(2):
            i = c + CH * b
            j = c + CH * (1 - b)
            dh = nt(g0[b], W[0, i, 0:BLK]) + nt(g0[1 - b], W[0, j, BLK:2 * BLK])
            dh0[c, b] = dh
            acc[...] += dh * normed(c, b)

        @pl.when(c >= 1)
        def _():
            rs_step1(c - 1)

        h2_copy(c).wait_recv()
        for b in range(2):
            i = c + CH * b
            ct = cot[:, cols(c, b)]
            put_grads(2 * CH + c, b, tn(h2[c, b], ct), tn(h2p[c, b], ct))
        rs_start(2 * CH + c)
        for b in range(2):
            i = c + CH * b
            pre = nn(h2[c, b], W[2, i, 0:BLK]) + nn(h2p[c, b], W[2, i, BLK:2 * BLK])
            mixed[:, cols(c, b)] = (tok[:, cols(c, b)].astype(F32) + pre).astype(BF16)

        @pl.when(c >= 1)
        def _():
            rs_step1(2 * CH + c - 1)

        @pl.when(c >= 2)
        def _():
            rs_step2(c - 2)
            rs_step2(2 * CH + c - 2)

    loop(phase2)
    put_stat(1, jnp.sum(acc[...], axis=1, keepdims=True))
    for o in range(1, n_z):
        stat_copy(1, o).start()
    rs_step1(CH - 1)
    rs_step1(3 * CH - 1)
    for c in (CH - 2, CH - 1):
        rs_step2(c)
        rs_step2(2 * CH + c)
    for o in range(1, n_z):
        stat_arrival(1, o).wait_recv()
    inner = get_stat(1) / D

    def finish(c):
        inv = invr[:, 0:1]
        for b in range(2):
            value = cot[:, cols(c, b)].astype(F32) + inv * (dh0[c, b] - normed(c, b) * inner)
            tg[:, cols(c, b)] = value.astype(BF16)

    loop(finish)

    def finish_grads(c):
        rs_finish(1, c)
        rs_finish(0, c)
        rs_finish(2, c)

    loop(finish_grads)

    for which in range(2):
        for o in range(1, n_z):
            stat_copy(which, o).wait_send()
    for k in (1, 2):
        far_weights(k).wait_send()
        for o in range(1, n_dp):
            spread(k, o).wait_send()

    def drain(c):
        for b in range(2):
            cot_copy(c, b).wait_send()
        h1_copy(c).wait_send()
        h2_copy(c).wait_send()
        g1_copy(c).wait_send()
        for k in range(FACTORS):
            j = CH * k + c
            for copy in [s0_copy(j)] + s1_copies(j) + s2_copies(j):
                copy.wait_send()

    loop(drain)


def shards(n_dp, n_z, tokens, weights, cotangent):
    tok_rows, local_width = tokens.shape
    blocks_dev = local_width // BLK
    assert blocks_dev == 2 * CH and n_z == 4 and n_dp % 8 == 0
    na = n_dp // 4
    rows = 2 * BLK // n_dp
    jobs = FACTORS * CH
    wt = jnp.transpose(weights, (0, 2, 1, 3))
    vm = pl.BlockSpec(memory_space=pltpu.VMEM)
    sem = pltpu.SemaphoreType.DMA
    pair = lambda kind: pltpu.VMEM((CH, 2, tok_rows, BLK), kind)
    twice = lambda *s: [sem(s), sem(s)]
    mixed, tg, wg = pl.pallas_call(
        functools.partial(kernel, n_dp, n_z),
        out_shape=(
            jax.ShapeDtypeStruct((tok_rows, local_width), BF16),
            jax.ShapeDtypeStruct((tok_rows, local_width), BF16),
            jax.ShapeDtypeStruct((FACTORS, blocks_dev, rows, BLK), F32),
        ),
        in_specs=[vm, vm, pl.BlockSpec(memory_space=pl.ANY)],
        out_specs=(vm, vm, vm),
        scratch_shapes=[
            pltpu.VMEM((FACTORS, blocks_dev, 2 * BLK, BLK), BF16),
            pltpu.VMEM((2, n_dp, 8 * BLK // n_dp, BLK), BF16),
            pair(BF16), pair(BF16), pair(BF16), pair(BF16), pair(BF16), pair(BF16),
            pair(BF16), pair(BF16), pair(F32), pair(F32), pair(F32),
            pltpu.VMEM((tok_rows, BLK), F32),
            pltpu.VMEM((tok_rows, 128), F32),
            pltpu.VMEM((jobs, 2, na, 2, 2, rows, BLK), F32),
            pltpu.VMEM((jobs, 2, na, 2, rows, BLK), F32),
            pltpu.VMEM((jobs, na, rows, BLK), F32),
            pltpu.VMEM((jobs, na - 1, 2, rows, BLK), F32),
            pltpu.VMEM((jobs, na - 1, rows, BLK), F32),
            pltpu.VMEM((jobs, rows, BLK), F32),
            pltpu.VMEM((2, n_z, 8, tok_rows), F32),
            sem(()),
        ]
        + twice(2, n_z - 1) + twice(2) + twice(2, n_dp - 1) + twice(CH, 2)
        + twice(CH) + twice(CH) + twice(CH)
        + twice(jobs) + twice(jobs) + twice(jobs, na - 1) + twice(jobs, na - 1) + twice(jobs),
        compiler_params=pltpu.CompilerParams(
            collective_id=0, has_side_effects=True, vmem_limit_bytes=60 * 1024 * 1024
        ),
        cost_estimate=pl.CostEstimate(
            flops=6 * FACTORS * 2 * tok_rows * blocks_dev * BLK * BLK,
            bytes_accessed=16 * 1024 * 1024, transcendentals=4 * tok_rows * local_width,
        ),
    )(tokens, cotangent, wt)
    return mixed, tg, jnp.transpose(wg, (0, 2, 1, 3))


def solution(mesh):
    return jax.shard_map(
        functools.partial(shards, mesh.shape["dp"], mesh.shape["tensor"]),
        mesh=mesh,
        in_specs=(P("dp", "tensor"), P(None, None, "tensor", None), P("dp", "tensor")),
        out_specs=(P("dp", "tensor"), P("dp", "tensor"), P(None, "dp", "tensor", None)),
        check_vma=False,
    )
```

```python
import functools
import math

import jax
import jax.numpy as jnp
from jax import lax
from jax.experimental import pallas as pl
from jax.experimental.pallas import tpu as pltpu
from jax.sharding import PartitionSpec as P

D = 8192
BLK = 256
FACTORS = 3
CH = 4

root_half = 0.7071067811865476
pdf_scale = 0.3989422804014327
epsilon = 1e-06
MESH = pl.DeviceIdType.MESH
F32 = jnp.float32
BF16 = jnp.bfloat16


def nn(a, b):
    return lax.dot_general(a, b, (((1,), (0,)), ((), ())), preferred_element_type=F32)


def nt(a, b):
    return lax.dot_general(a, b, (((1,), (1,)), ((), ())), preferred_element_type=F32)


def tn(a, b):
    return lax.dot_general(a, b, (((0,), (0,)), ((), ())), preferred_element_type=F32)


def gelu_and_slope(value):
    cdf = 0.5 * (1.0 + lax.erf(value * root_half))
    return value * cdf, cdf + value * jnp.exp(-0.5 * value * value) * pdf_scale


def kernel(
    n_dp, n_z, tok, cot, wt, mixed, tg, wg,
    W, Wfp, cotp, h0, h1, h1p, h2, h2p, g1, g1p, sl0, sl1, dh0, acc, invr,
    A, R0, R1a, R1b, R2a, R2b, red, stat,
    wsem, st_s, st_r, wz_s, wz_r, wb_s, wb_r, ct_s, ct_r,
    h1_s, h1_r, h2_s, h2_r, g1_s, g1_r,
    s0_s, s0_r, s1a_s, s1a_r, s1b_s, s1b_r, s2a_s, s2a_r, s2b_s, s2b_r,
):
    na = n_dp // 4
    rows = 2 * BLK // n_dp
    wrows = 8 * BLK // n_dp
    per_block = n_dp // 8
    d = lax.axis_index("dp")
    z = lax.axis_index("tensor")
    da = d // 4
    dx = (d // 2) % 2
    dc = d % 2
    grad_scale = 1.0 / math.sqrt(tok.shape[0] * n_dp)
    tok_rows = tok.shape[0]

    def xor(v, o):
        out = v
        bit = 1
        while bit <= o:
            if o & bit:
                out = out + bit - 2 * bit * ((v // bit) % 2)
            bit *= 2
        return out

    zp = {1: xor(z, 1), 2: xor(z, 2)}

    def remote(src, dst, s, r, where):
        return pltpu.make_async_remote_copy(
            src_ref=src, dst_ref=dst, send_sem=s, recv_sem=r,
            device_id=where, device_id_type=MESH,
        )

    wload = pltpu.make_async_copy(wt, W, wsem)
    wload.start()

    def stat_copy(which, o):
        return remote(
            stat.at[which, z], stat.at[which, z],
            st_s.at[which, o - 1], st_r.at[which, o - 1], {"tensor": xor(z, o)},
        )

    def stat_arrival(which, o):
        zo = xor(z, o)
        return remote(
            stat.at[which, zo], stat.at[which, zo],
            st_s.at[which, o - 1], st_r.at[which, o - 1], {"tensor": zo},
        )

    def put_stat(which, column):
        wide = jnp.broadcast_to(column, (tok_rows, 128))
        stat[which, z] = jnp.transpose(wide)[0:8]

    def get_stat(which):
        total = stat[which, 0]
        for i in range(1, n_z):
            total = total + stat[which, i]
        wide = jnp.broadcast_to(total[0:1], (128, tok_rows))
        return jnp.transpose(wide)[:, 0:1]

    part = jnp.zeros((tok_rows, BLK), F32)
    for i in range(2 * CH):
        x = tok[:, i * BLK:(i + 1) * BLK].astype(F32)
        part = part + x * x
    put_stat(0, jnp.sum(part, axis=1, keepdims=True))

    barrier = pltpu.get_barrier_semaphore()
    for o in range(1, n_z):
        pl.semaphore_signal(barrier, inc=1, device_id={"tensor": xor(z, o)}, device_id_type=MESH)
    for o in range(1, n_dp):
        pl.semaphore_signal(barrier, inc=1, device_id={"dp": xor(d, o)}, device_id_type=MESH)
    pl.semaphore_wait(barrier, n_z + n_dp - 2)

    for o in range(1, n_z):
        stat_copy(0, o).start()

    def far_weights(k):
        return remote(
            wt.at[k, d // per_block,
                  pl.ds(pl.multiple_of(BLK + (d % per_block) * wrows, wrows), wrows)],
            Wfp.at[k - 1, d], wz_s.at[k - 1], wz_r.at[k - 1], {"tensor": zp[k]},
        )

    far_weights(2).start()

    def cols(c, b):
        return pl.ds(pl.multiple_of((c + CH * b) * BLK, BLK), BLK)

    def cot_copy(c, b):
        return remote(cot.at[:, cols(c, b)], cotp.at[c, b],
                      ct_s.at[c, b], ct_r.at[c, b], {"tensor": zp[2]})

    for c in range(CH // 2):
        for b in range(2):
            cot_copy(c, b).start()

    def h1_copy(c):
        return remote(h1.at[c], h1p.at[c], h1_s.at[c], h1_r.at[c], {"tensor": zp[1]})

    def h2_copy(c):
        return remote(h2.at[c], h2p.at[c], h2_s.at[c], h2_r.at[c], {"tensor": zp[2]})

    def g1_copy(c):
        return remote(g1.at[c], g1p.at[c], g1_s.at[c], g1_r.at[c], {"tensor": zp[1]})

    def s0_copy(j):
        return remote(A.at[j, :, :, :, 1 - dc], R0.at[j], s0_s.at[j], s0_r.at[j],
                      {"dp": xor(d, 1)})

    def s1_copies(j):
        out = [remote(A.at[j, 0, :, 1 - dx, dc], R1a.at[j], s1a_s.at[j], s1a_r.at[j],
                      {"dp": xor(d, 2)})]
        for o in range(1, na):
            out.append(remote(A.at[j, 1, xor(da, o), :, dc], R1b.at[j, o - 1],
                              s1b_s.at[j, o - 1], s1b_r.at[j, o - 1], {"dp": xor(d, 4 * o)}))
        return out

    def s2_copies(j):
        out = [remote(A.at[j, 1, da, 1 - dx, dc], R2b.at[j], s2b_s.at[j], s2b_r.at[j],
                      {"dp": xor(d, 2)})]
        for o in range(1, na):
            out.append(remote(A.at[j, 0, xor(da, o), dx, dc], R2a.at[j, o - 1],
                              s2a_s.at[j, o - 1], s2a_r.at[j, o - 1], {"dp": xor(d, 4 * o)}))
        return out

    def rs_start(j):
        s0_copy(j).start()

    def rs_step1(j):
        s0_copy(j).wait_recv()
        A[j, :, :, :, dc] = A[j, :, :, :, dc] + R0[j]
        for copy in s1_copies(j):
            copy.start()

    def rs_step2(j):
        for copy in s1_copies(j):
            copy.wait_recv()
        A[j, 0, :, dx, dc] = A[j, 0, :, dx, dc] + R1a[j]
        total = A[j, 1, da, :, dc]
        for o in range(1, na):
            total = total + R1b[j, o - 1]
        A[j, 1, da, :, dc] = total
        for copy in s2_copies(j):
            copy.start()

    def rs_finish(k, c):
        j = CH * k + c
        for copy in s2_copies(j):
            copy.wait_recv()
        total = A[j, 0, da, dx, dc]
        for o in range(1, na):
            total = total + R2a[j, o - 1]
        red[k, c] = total * grad_scale
        red[k, c + CH] = (A[j, 1, da, dx, dc] + R2b[j]) * grad_scale

    def put_grads(j, b, near, far):
        A[j, b, 0:na // 2] = near.reshape(na // 2, 2, 2, rows, BLK)
        A[j, b, na // 2:na] = far.reshape(na // 2, 2, 2, rows, BLK)

    wload.wait()
    for o in range(1, n_z):
        stat_arrival(0, o).wait_recv()
    invr[...] = jnp.broadcast_to(lax.rsqrt(get_stat(0) / D + epsilon), (tok_rows, 128))

    def normed(c, b):
        return tok[:, cols(c, b)].astype(F32) * invr[:, 0:1]

    def loop(body):
        def step(c, carry):
            body(c)
            return carry
        lax.fori_loop(0, CH, step, 0)

    def phase0(c):
        for b in range(2):
            h0[c, b] = normed(c, b).astype(BF16)
        for b in range(2):
            i = c + CH * b
            pre = nn(h0[c, b], W[0, i, 0:BLK]) + nn(h0[c, 1 - b], W[0, i, BLK:2 * BLK])
            value, slope = gelu_and_slope(pre)
            h1[c, b] = value.astype(BF16)
            sl0[c, b] = slope
        h1_copy(c).start()

    loop(phase0)
    for c in range(CH // 2, CH):
        for b in range(2):
            cot_copy(c, b).start()
    far_weights(1).start()

    def spread(k, o):
        return remote(Wfp.at[k - 1, d], Wfp.at[k - 1, d],
                      wb_s.at[k - 1, o - 1], wb_r.at[k - 1, o - 1], {"dp": xor(d, o)})

    def spread_arrival(k, o):
        other = xor(d, o)
        return remote(Wfp.at[k - 1, other], Wfp.at[k - 1, other],
                      wb_s.at[k - 1, o - 1], wb_r.at[k - 1, o - 1], {"dp": other})

    def spread_out(k):
        far_weights(k).wait_recv()
        for o in range(1, n_dp):
            spread(k, o).start()

    spread_out(2)

    def far_block(k, i):
        return Wfp[k - 1, pl.ds(i * per_block, per_block)].reshape(BLK, BLK)

    for o in range(1, n_dp):
        spread_arrival(2, o).wait_recv()

    def phase1(c):
        h1_copy(c).wait_recv()
        for b in range(2):
            i = c + CH * b
            pre = nn(h1[c, b], W[1, i, 0:BLK]) + nn(h1p[c, b], W[1, i, BLK:2 * BLK])
            value, slope = gelu_and_slope(pre)
            h2[c, b] = value.astype(BF16)
            sl1[c, b] = slope
        for b in range(2):
            i = c + CH * b
            cot_copy(c, b).wait_recv()
            dh = nt(cot[:, cols(c, b)], W[2, i, 0:BLK]) + nt(cotp[c, b], far_block(2, i))
            g1[c, b] = (dh * sl1[c, b]).astype(BF16)
        g1_copy(c).start()
        h2_copy(c).start()
        for b in range(2):
            put_grads(CH + c, b, tn(h1[c, b], g1[c, b]), tn(h1p[c, b], g1[c, b]))
        rs_start(CH + c)

        @pl.when(c >= 1)
        def _():
            rs_step1(CH + c - 1)

        @pl.when(c == 1)
        def _():
            spread_out(1)

    loop(phase1)
    rs_step1(CH + CH - 1)
    for o in range(1, n_dp):
        spread_arrival(1, o).wait_recv()
    acc[...] = jnp.zeros_like(acc)

    def phase2(c):
        rs_step2(CH + c)
        g1_copy(c).wait_recv()
        g0 = []
        for b in range(2):
            i = c + CH * b
            dh = nt(g1[c, b], W[1, i, 0:BLK]) + nt(g1p[c, b], far_block(1, i))
            g0.append((dh * sl0[c, b]).astype(BF16))
        for b in range(2):
            put_grads(c, b, tn(h0[c, b], g0[b]), tn(h0[c, 1 - b], g0[b]))
        rs_start(c)
        for b in range(2):
            i = c + CH * b
            j = c + CH * (1 - b)
            dh = nt(g0[b], W[0, i, 0:BLK]) + nt(g0[1 - b], W[0, j, BLK:2 * BLK])
            dh0[c, b] = dh
            acc[...] += dh * normed(c, b)

        @pl.when(c >= 1)
        def _():
            rs_step1(c - 1)

    loop(phase2)
    put_stat(1, jnp.sum(acc[...], axis=1, keepdims=True))
    for o in range(1, n_z):
        stat_copy(1, o).start()
    rs_step1(CH - 1)

    def phase3(c):
        rs_step2(c)
        rs_finish(1, c)
        h2_copy(c).wait_recv()
        for b in range(2):
            ct = cot[:, cols(c, b)]
            put_grads(2 * CH + c, b, tn(h2[c, b], ct), tn(h2p[c, b], ct))
        rs_start(2 * CH + c)
        for b in range(2):
            i = c + CH * b
            pre = nn(h2[c, b], W[2, i, 0:BLK]) + nn(h2p[c, b], W[2, i, BLK:2 * BLK])
            mixed[:, cols(c, b)] = (tok[:, cols(c, b)].astype(F32) + pre).astype(BF16)

        @pl.when(c >= 1)
        def _():
            rs_step1(2 * CH + c - 1)

        @pl.when(c >= 2)
        def _():
            rs_step2(2 * CH + c - 2)

    loop(phase3)
    rs_step1(3 * CH - 1)
    for o in range(1, n_z):
        stat_arrival(1, o).wait_recv()
    inner = get_stat(1) / D

    def finish(c):
        inv = invr[:, 0:1]
        for b in range(2):
            value = cot[:, cols(c, b)].astype(F32) + inv * (dh0[c, b] - normed(c, b) * inner)
            tg[:, cols(c, b)] = value.astype(BF16)

    loop(finish)
    rs_step2(3 * CH - 2)
    rs_step2(3 * CH - 1)

    loop(lambda c: rs_finish(0, c))
    for k in range(2):
        wg[k] = jnp.transpose(red[k], (1, 0, 2))
    loop(lambda c: rs_finish(2, c))
    wg[2] = jnp.transpose(red[2], (1, 0, 2))

    for which in range(2):
        for o in range(1, n_z):
            stat_copy(which, o).wait_send()
    for k in (1, 2):
        far_weights(k).wait_send()
        for o in range(1, n_dp):
            spread(k, o).wait_send()

    def drain(c):
        for b in range(2):
            cot_copy(c, b).wait_send()
        h1_copy(c).wait_send()
        h2_copy(c).wait_send()
        g1_copy(c).wait_send()
        for k in range(FACTORS):
            j = CH * k + c
            for copy in [s0_copy(j)] + s1_copies(j) + s2_copies(j):
                copy.wait_send()

    loop(drain)


def hand_over(a, b, c, a_out, b_out, c_out, sems):
    copies = [
        pltpu.make_async_copy(src, dst, sems.at[i])
        for i, (src, dst) in enumerate(((a, a_out), (b, b_out), (c, c_out)))
    ]
    for copy in copies:
        copy.start()
    for copy in copies:
        copy.wait()


def shards(n_dp, n_z, tokens, weights, cotangent):
    tok_rows, local_width = tokens.shape
    blocks_dev = local_width // BLK
    assert blocks_dev == 2 * CH and n_z == 4 and n_dp % 8 == 0
    na = n_dp // 4
    rows = 2 * BLK // n_dp
    jobs = FACTORS * CH
    wt = jnp.transpose(weights, (0, 2, 1, 3))
    vm = pl.BlockSpec(memory_space=pltpu.VMEM)
    sem = pltpu.SemaphoreType.DMA
    pair = lambda kind: pltpu.VMEM((CH, 2, tok_rows, BLK), kind)
    twice = lambda *s: [sem(s), sem(s)]
    outs = pl.pallas_call(
        functools.partial(kernel, n_dp, n_z),
        out_shape=(
            jax.ShapeDtypeStruct((tok_rows, local_width), BF16),
            jax.ShapeDtypeStruct((tok_rows, local_width), BF16),
            jax.ShapeDtypeStruct((FACTORS, rows, blocks_dev, BLK), F32),
        ),
        in_specs=[vm, vm, pl.BlockSpec(memory_space=pl.ANY)],
        out_specs=(vm, vm, vm),
        scratch_shapes=[
            pltpu.VMEM((FACTORS, blocks_dev, 2 * BLK, BLK), BF16),
            pltpu.VMEM((2, n_dp, 8 * BLK // n_dp, BLK), BF16),
            pair(BF16), pair(BF16), pair(BF16), pair(BF16), pair(BF16), pair(BF16),
            pair(BF16), pair(BF16), pair(F32), pair(F32), pair(F32),
            pltpu.VMEM((tok_rows, BLK), F32),
            pltpu.VMEM((tok_rows, 128), F32),
            pltpu.VMEM((jobs, 2, na, 2, 2, rows, BLK), F32),
            pltpu.VMEM((jobs, 2, na, 2, rows, BLK), F32),
            pltpu.VMEM((jobs, na, rows, BLK), F32),
            pltpu.VMEM((jobs, na - 1, 2, rows, BLK), F32),
            pltpu.VMEM((jobs, na - 1, rows, BLK), F32),
            pltpu.VMEM((jobs, rows, BLK), F32),
            pltpu.VMEM((FACTORS, blocks_dev, rows, BLK), F32),
            pltpu.VMEM((2, n_z, 8, tok_rows), F32),
            sem(()),
        ]
        + twice(2, n_z - 1) + twice(2) + twice(2, n_dp - 1) + twice(CH, 2)
        + twice(CH) + twice(CH) + twice(CH)
        + twice(jobs) + twice(jobs) + twice(jobs, na - 1) + twice(jobs, na - 1) + twice(jobs),
        compiler_params=pltpu.CompilerParams(
            collective_id=0, has_side_effects=True, vmem_limit_bytes=60 * 1024 * 1024
        ),
        cost_estimate=pl.CostEstimate(
            flops=6 * FACTORS * 2 * tok_rows * blocks_dev * BLK * BLK,
            bytes_accessed=16 * 1024 * 1024, transcendentals=4 * tok_rows * local_width,
        ),
    )(tokens, cotangent, wt)
    hbm = pl.BlockSpec(memory_space=pl.ANY)
    return tuple(pl.pallas_call(
        hand_over,
        out_shape=[jax.ShapeDtypeStruct(x.shape, x.dtype) for x in outs],
        in_specs=[hbm] * 3,
        out_specs=[hbm] * 3,
        scratch_shapes=[sem((3,))],
    )(*outs))


def solution(mesh):
    return jax.shard_map(
        functools.partial(shards, mesh.shape["dp"], mesh.shape["tensor"]),
        mesh=mesh,
        in_specs=(P("dp", "tensor"), P(None, None, "tensor", None), P("dp", "tensor")),
        out_specs=(P("dp", "tensor"), P("dp", "tensor"), P(None, "dp", "tensor", None)),
        check_vma=False,
    )
```

```python
import functools
import math

import jax
import jax.numpy as jnp
from jax import lax
from jax.experimental import pallas as pl
from jax.experimental.pallas import tpu as pltpu
from jax.sharding import PartitionSpec as P

D = 8192
BLK = 256
FACTORS = 3
CH = 4

root_half = 0.7071067811865476
pdf_scale = 0.3989422804014327
epsilon = 1e-06
MESH = pl.DeviceIdType.MESH
F32 = jnp.float32
BF16 = jnp.bfloat16


def nn(a, b):
    return lax.dot_general(a, b, (((1,), (0,)), ((), ())), preferred_element_type=F32)


def nt(a, b):
    return lax.dot_general(a, b, (((1,), (1,)), ((), ())), preferred_element_type=F32)


def tn(a, b):
    return lax.dot_general(a, b, (((0,), (0,)), ((), ())), preferred_element_type=F32)


def gelu_and_slope(value):
    cdf = 0.5 * (1.0 + lax.erf(value * root_half))
    return value * cdf, cdf + value * jnp.exp(-0.5 * value * value) * pdf_scale


def kernel(
    n_dp, n_z, tok, cot, wt, mixed, tg, wg,
    W, Wfp, cotp, h0, h1, h1p, h2, h2p, g1, g1p, sl0, sl1, dh0, acc, invr,
    A, R0, R1a, R1b, R2a, R2b, stat,
    wsem, st_s, st_r, wz_s, wz_r, wb_s, wb_r, ct_s, ct_r,
    h1_s, h1_r, h2_s, h2_r, g1_s, g1_r,
    s0_s, s0_r, s1a_s, s1a_r, s1b_s, s1b_r, s2a_s, s2a_r, s2b_s, s2b_r,
):
    na = n_dp // 4
    rows = 2 * BLK // n_dp
    wrows = 8 * BLK // n_dp
    per_block = n_dp // 8
    d = lax.axis_index("dp")
    z = lax.axis_index("tensor")
    da = d // 4
    dx = (d // 2) % 2
    dc = d % 2
    grad_scale = 1.0 / math.sqrt(tok.shape[0] * n_dp)
    tok_rows = tok.shape[0]

    def xor(v, o):
        out = v
        bit = 1
        while bit <= o:
            if o & bit:
                out = out + bit - 2 * bit * ((v // bit) % 2)
            bit *= 2
        return out

    zp = {1: xor(z, 1), 2: xor(z, 2)}

    def remote(src, dst, s, r, where):
        return pltpu.make_async_remote_copy(
            src_ref=src, dst_ref=dst, send_sem=s, recv_sem=r,
            device_id=where, device_id_type=MESH,
        )

    wload = pltpu.make_async_copy(wt, W, wsem)
    wload.start()

    def stat_copy(which, o):
        return remote(
            stat.at[which, z], stat.at[which, z],
            st_s.at[which, o - 1], st_r.at[which, o - 1], {"tensor": xor(z, o)},
        )

    def stat_arrival(which, o):
        zo = xor(z, o)
        return remote(
            stat.at[which, zo], stat.at[which, zo],
            st_s.at[which, o - 1], st_r.at[which, o - 1], {"tensor": zo},
        )

    def put_stat(which, column):
        wide = jnp.broadcast_to(column, (tok_rows, 128))
        stat[which, z] = jnp.transpose(wide)[0:8]

    def get_stat(which):
        total = stat[which, 0]
        for i in range(1, n_z):
            total = total + stat[which, i]
        wide = jnp.broadcast_to(total[0:1], (128, tok_rows))
        return jnp.transpose(wide)[:, 0:1]

    part = jnp.zeros((tok_rows, BLK), F32)
    for i in range(2 * CH):
        x = tok[:, i * BLK:(i + 1) * BLK].astype(F32)
        part = part + x * x
    put_stat(0, jnp.sum(part, axis=1, keepdims=True))

    barrier = pltpu.get_barrier_semaphore()
    for o in range(1, n_z):
        pl.semaphore_signal(barrier, inc=1, device_id={"tensor": xor(z, o)}, device_id_type=MESH)
    for o in range(1, n_dp):
        pl.semaphore_signal(barrier, inc=1, device_id={"dp": xor(d, o)}, device_id_type=MESH)
    pl.semaphore_wait(barrier, n_z + n_dp - 2)

    for o in range(1, n_z):
        stat_copy(0, o).start()

    def far_weights(k):
        return remote(
            wt.at[k, d // per_block,
                  pl.ds(pl.multiple_of(BLK + (d % per_block) * wrows, wrows), wrows)],
            Wfp.at[k - 1, d], wz_s.at[k - 1], wz_r.at[k - 1], {"tensor": zp[k]},
        )

    far_weights(2).start()
    far_weights(1).start()

    def cols(c, b):
        return pl.ds(pl.multiple_of((c + CH * b) * BLK, BLK), BLK)

    def cot_copy(c, b):
        return remote(cot.at[:, cols(c, b)], cotp.at[c, b],
                      ct_s.at[c, b], ct_r.at[c, b], {"tensor": zp[2]})

    for c in range(CH):
        for b in range(2):
            cot_copy(c, b).start()

    def h1_copy(c):
        return remote(h1.at[c], h1p.at[c], h1_s.at[c], h1_r.at[c], {"tensor": zp[1]})

    def h2_copy(c):
        return remote(h2.at[c], h2p.at[c], h2_s.at[c], h2_r.at[c], {"tensor": zp[2]})

    def g1_copy(c):
        return remote(g1.at[c], g1p.at[c], g1_s.at[c], g1_r.at[c], {"tensor": zp[1]})

    def s0_copy(j):
        return remote(A.at[j, :, :, :, 1 - dc], R0.at[j], s0_s.at[j], s0_r.at[j],
                      {"dp": xor(d, 1)})

    def s1_copies(j):
        out = [remote(A.at[j, 0, :, 1 - dx, dc], R1a.at[j], s1a_s.at[j], s1a_r.at[j],
                      {"dp": xor(d, 2)})]
        for o in range(1, na):
            out.append(remote(A.at[j, 1, xor(da, o), :, dc], R1b.at[j, o - 1],
                              s1b_s.at[j, o - 1], s1b_r.at[j, o - 1], {"dp": xor(d, 4 * o)}))
        return out

    def s2_copies(j):
        out = [remote(A.at[j, 1, da, 1 - dx, dc], R2b.at[j], s2b_s.at[j], s2b_r.at[j],
                      {"dp": xor(d, 2)})]
        for o in range(1, na):
            out.append(remote(A.at[j, 0, xor(da, o), dx, dc], R2a.at[j, o - 1],
                              s2a_s.at[j, o - 1], s2a_r.at[j, o - 1], {"dp": xor(d, 4 * o)}))
        return out

    def rs_start(j):
        s0_copy(j).start()

    def rs_step1(j):
        s0_copy(j).wait_recv()
        A[j, :, :, :, dc] = A[j, :, :, :, dc] + R0[j]
        for copy in s1_copies(j):
            copy.start()

    def rs_step2(j):
        for copy in s1_copies(j):
            copy.wait_recv()
        A[j, 0, :, dx, dc] = A[j, 0, :, dx, dc] + R1a[j]
        total = A[j, 1, da, :, dc]
        for o in range(1, na):
            total = total + R1b[j, o - 1]
        A[j, 1, da, :, dc] = total
        for copy in s2_copies(j):
            copy.start()

    def rs_finish(k, c):
        j = CH * k + c
        for copy in s2_copies(j):
            copy.wait_recv()
        total = A[j, 0, da, dx, dc]
        for o in range(1, na):
            total = total + R2a[j, o - 1]
        wg[k, :, c] = total * grad_scale
        wg[k, :, c + CH] = (A[j, 1, da, dx, dc] + R2b[j]) * grad_scale

    def put_grads(j, b, near, far):
        A[j, b, 0:na // 2] = near.reshape(na // 2, 2, 2, rows, BLK)
        A[j, b, na // 2:na] = far.reshape(na // 2, 2, 2, rows, BLK)

    wload.wait()
    for o in range(1, n_z):
        stat_arrival(0, o).wait_recv()
    invr[...] = jnp.broadcast_to(lax.rsqrt(get_stat(0) / D + epsilon), (tok_rows, 128))

    def normed(c, b):
        return tok[:, cols(c, b)].astype(F32) * invr[:, 0:1]

    def loop(body):
        def step(c, carry):
            body(c)
            return carry
        lax.fori_loop(0, CH, step, 0)

    def phase0(c):
        for b in range(2):
            h0[c, b] = normed(c, b).astype(BF16)
        for b in range(2):
            i = c + CH * b
            pre = nn(h0[c, b], W[0, i, 0:BLK]) + nn(h0[c, 1 - b], W[0, i, BLK:2 * BLK])
            value, slope = gelu_and_slope(pre)
            h1[c, b] = value.astype(BF16)
            sl0[c, b] = slope
        h1_copy(c).start()

    loop(phase0)

    def spread(k, o):
        return remote(Wfp.at[k - 1, d], Wfp.at[k - 1, d],
                      wb_s.at[k - 1, o - 1], wb_r.at[k - 1, o - 1], {"dp": xor(d, o)})

    def spread_arrival(k, o):
        other = xor(d, o)
        return remote(Wfp.at[k - 1, other], Wfp.at[k - 1, other],
                      wb_s.at[k - 1, o - 1], wb_r.at[k - 1, o - 1], {"dp": other})

    for k in (2, 1):
        far_weights(k).wait_recv()
        for o in range(1, n_dp):
            spread(k, o).start()

    def far_block(k, i):
        return Wfp[k - 1, pl.ds(i * per_block, per_block)].reshape(BLK, BLK)

    for o in range(1, n_dp):
        spread_arrival(2, o).wait_recv()

    def phase1(c):
        h1_copy(c).wait_recv()
        for b in range(2):
            i = c + CH * b
            pre = nn(h1[c, b], W[1, i, 0:BLK]) + nn(h1p[c, b], W[1, i, BLK:2 * BLK])
            value, slope = gelu_and_slope(pre)
            h2[c, b] = value.astype(BF16)
            sl1[c, b] = slope
        h2_copy(c).start()
        for b in range(2):
            i = c + CH * b
            cot_copy(c, b).wait_recv()
            dh = nt(cot[:, cols(c, b)], W[2, i, 0:BLK]) + nt(cotp[c, b], far_block(2, i))
            g1[c, b] = (dh * sl1[c, b]).astype(BF16)
        g1_copy(c).start()
        for b in range(2):
            put_grads(CH + c, b, tn(h1[c, b], g1[c, b]), tn(h1p[c, b], g1[c, b]))
        rs_start(CH + c)

        @pl.when(c >= 1)
        def _():
            rs_step1(CH + c - 1)

    loop(phase1)
    rs_step1(CH + CH - 1)
    for o in range(1, n_dp):
        spread_arrival(1, o).wait_recv()
    acc[...] = jnp.zeros_like(acc)

    def phase2(c):
        rs_step2(CH + c)
        g1_copy(c).wait_recv()
        g0 = []
        for b in range(2):
            i = c + CH * b
            dh = nt(g1[c, b], W[1, i, 0:BLK]) + nt(g1p[c, b], far_block(1, i))
            g0.append((dh * sl0[c, b]).astype(BF16))
        for b in range(2):
            put_grads(c, b, tn(h0[c, b], g0[b]), tn(h0[c, 1 - b], g0[b]))
        rs_start(c)
        for b in range(2):
            i = c + CH * b
            j = c + CH * (1 - b)
            dh = nt(g0[b], W[0, i, 0:BLK]) + nt(g0[1 - b], W[0, j, BLK:2 * BLK])
            dh0[c, b] = dh
            acc[...] += dh * normed(c, b)

        @pl.when(c >= 1)
        def _():
            rs_step1(c - 1)

        h2_copy(c).wait_recv()
        for b in range(2):
            i = c + CH * b
            ct = cot[:, cols(c, b)]
            put_grads(2 * CH + c, b, tn(h2[c, b], ct), tn(h2p[c, b], ct))
        rs_start(2 * CH + c)
        for b in range(2):
            i = c + CH * b
            pre = nn(h2[c, b], W[2, i, 0:BLK]) + nn(h2p[c, b], W[2, i, BLK:2 * BLK])
            mixed[:, cols(c, b)] = (tok[:, cols(c, b)].astype(F32) + pre).astype(BF16)

        @pl.when(c >= 1)
        def _():
            rs_step1(2 * CH + c - 1)

        @pl.when(c >= 2)
        def _():
            rs_step2(c - 2)
            rs_step2(2 * CH + c - 2)

    loop(phase2)
    put_stat(1, jnp.sum(acc[...], axis=1, keepdims=True))
    for o in range(1, n_z):
        stat_copy(1, o).start()
    rs_step1(CH - 1)
    rs_step1(3 * CH - 1)
    for c in (CH - 2, CH - 1):
        rs_step2(c)
        rs_step2(2 * CH + c)
    for o in range(1, n_z):
        stat_arrival(1, o).wait_recv()
    inner = get_stat(1) / D

    def finish(c):
        inv = invr[:, 0:1]
        for b in range(2):
            value = cot[:, cols(c, b)].astype(F32) + inv * (dh0[c, b] - normed(c, b) * inner)
            tg[:, cols(c, b)] = value.astype(BF16)

    loop(finish)

    def finish_grads(c):
        rs_finish(1, c)
        rs_finish(0, c)
        rs_finish(2, c)

    loop(finish_grads)

    for which in range(2):
        for o in range(1, n_z):
            stat_copy(which, o).wait_send()
    for k in (1, 2):
        far_weights(k).wait_send()
        for o in range(1, n_dp):
            spread(k, o).wait_send()

    def drain(c):
        for b in range(2):
            cot_copy(c, b).wait_send()
        h1_copy(c).wait_send()
        h2_copy(c).wait_send()
        g1_copy(c).wait_send()
        for k in range(FACTORS):
            j = CH * k + c
            for copy in [s0_copy(j)] + s1_copies(j) + s2_copies(j):
                copy.wait_send()

    loop(drain)


def hand_over(a, b, c, a_out, b_out, c_out, sems):
    copies = [
        pltpu.make_async_copy(src, dst, sems.at[i])
        for i, (src, dst) in enumerate(((a, a_out), (b, b_out), (c, c_out)))
    ]
    for copy in copies:
        copy.start()
    for copy in copies:
        copy.wait()


def shards(n_dp, n_z, tokens, weights, cotangent):
    tok_rows, local_width = tokens.shape
    blocks_dev = local_width // BLK
    assert blocks_dev == 2 * CH and n_z == 4 and n_dp % 8 == 0
    na = n_dp // 4
    rows = 2 * BLK // n_dp
    jobs = FACTORS * CH
    wt = jnp.transpose(weights, (0, 2, 1, 3))
    vm = pl.BlockSpec(memory_space=pltpu.VMEM)
    sem = pltpu.SemaphoreType.DMA
    pair = lambda kind: pltpu.VMEM((CH, 2, tok_rows, BLK), kind)
    twice = lambda *s: [sem(s), sem(s)]
    outs = pl.pallas_call(
        functools.partial(kernel, n_dp, n_z),
        out_shape=(
            jax.ShapeDtypeStruct((tok_rows, local_width), BF16),
            jax.ShapeDtypeStruct((tok_rows, local_width), BF16),
            jax.ShapeDtypeStruct((FACTORS, rows, blocks_dev, BLK), F32),
        ),
        in_specs=[vm, vm, pl.BlockSpec(memory_space=pl.ANY)],
        out_specs=(vm, vm, vm),
        scratch_shapes=[
            pltpu.VMEM((FACTORS, blocks_dev, 2 * BLK, BLK), BF16),
            pltpu.VMEM((2, n_dp, 8 * BLK // n_dp, BLK), BF16),
            pair(BF16), pair(BF16), pair(BF16), pair(BF16), pair(BF16), pair(BF16),
            pair(BF16), pair(BF16), pair(F32), pair(F32), pair(F32),
            pltpu.VMEM((tok_rows, BLK), F32),
            pltpu.VMEM((tok_rows, 128), F32),
            pltpu.VMEM((jobs, 2, na, 2, 2, rows, BLK), F32),
            pltpu.VMEM((jobs, 2, na, 2, rows, BLK), F32),
            pltpu.VMEM((jobs, na, rows, BLK), F32),
            pltpu.VMEM((jobs, na - 1, 2, rows, BLK), F32),
            pltpu.VMEM((jobs, na - 1, rows, BLK), F32),
            pltpu.VMEM((jobs, rows, BLK), F32),
            pltpu.VMEM((2, n_z, 8, tok_rows), F32),
            sem(()),
        ]
        + twice(2, n_z - 1) + twice(2) + twice(2, n_dp - 1) + twice(CH, 2)
        + twice(CH) + twice(CH) + twice(CH)
        + twice(jobs) + twice(jobs) + twice(jobs, na - 1) + twice(jobs, na - 1) + twice(jobs),
        compiler_params=pltpu.CompilerParams(
            collective_id=0, has_side_effects=True, vmem_limit_bytes=60 * 1024 * 1024
        ),
        cost_estimate=pl.CostEstimate(
            flops=6 * FACTORS * 2 * tok_rows * blocks_dev * BLK * BLK,
            bytes_accessed=16 * 1024 * 1024, transcendentals=4 * tok_rows * local_width,
        ),
    )(tokens, cotangent, wt)
    hbm = pl.BlockSpec(memory_space=pl.ANY)
    return tuple(pl.pallas_call(
        hand_over,
        out_shape=[jax.ShapeDtypeStruct(x.shape, x.dtype) for x in outs],
        in_specs=[vm] * 3,
        out_specs=[hbm] * 3,
        scratch_shapes=[sem((3,))],
    )(*outs))


def solution(mesh):
    return jax.shard_map(
        functools.partial(shards, mesh.shape["dp"], mesh.shape["tensor"]),
        mesh=mesh,
        in_specs=(P("dp", "tensor"), P(None, None, "tensor", None), P("dp", "tensor")),
        out_specs=(P("dp", "tensor"), P("dp", "tensor"), P(None, "dp", "tensor", None)),
        check_vma=False,
    )
```
